128 devices in a mesh: depth: 8 (over z, core), rows: 16 (over y, x).
Axes of the slice: x: 4, y: 4, z: 4, core: 2. Of those that a mesh axis runs over, the one named last changes fastest.
Arguments:
- density: float32 [128, 2048, 2048], P('depth', 'rows'), may hold values from 0.2 to 3
- occupancy: int32 [8, 16, 16], P('depth', 'rows'), may hold values from 0 to 1, as said below
- transfer: float32 [2, 4], replicated, may hold values from -1.5 to 1.5
Outputs:
- image: float32 [4, 2048, 2048], P(None, 'rows', 'depth')
The draws below stay inside these ranges and needn't reach their ends.
Inputs may be any that keep to these rules, and one draw needn't show every extreme that they name: `occupancy`: each entry is 0 or 1 and flags a block of 16 x 128 x 128 cells as occupied; at most 12 of the blocks of one device's brick are occupied, and some brick has exactly 12.
All inputs are finite; a program needn't handle non-finite values.
Results may differ from the reference program's by a relative error of at most 0.000079.
Values sent between devices are 32-bit elements; how exact they have to be, the bound alone decides.
A program may use at most 256 MiB of HBM per device.

```python
import math
import jax
import jax.numpy as jnp
from jax import lax

BZ = 16
BY = 128
NX = 2048
CB = 128
OCCMAX = 12
NZ = 128
NY = 2048


def draw_occupancy(key, part):
    brick_count = NZ // BZ * (NY // BY)
    block_count = NX // CB
    first_key, second_key, third_key = jax.random.split(key, 3)
    counts = jax.random.randint(first_key, (brick_count,), max(OCCMAX // 3, 1), OCCMAX + 1)
    full_brick = jax.random.randint(second_key, (), 0, brick_count)
    counts = jnp.where(jnp.arange(brick_count) == full_brick, OCCMAX, counts)
    scores = jax.random.randint(third_key, (brick_count, block_count), 0, 1 << 20) * block_count + jnp.arange(block_count)
    ranks = jnp.argsort(jnp.argsort(scores, axis=1), axis=1)
    flags = (ranks < counts[:, None]).astype(jnp.int32)
    return flags.reshape(NZ // BZ, NY // BY, block_count)


def block_levels(stream_key, dims, cuts, smallest, high):
    level, own = 1.0, jax.random.fold_in(stream_key, 6)
    for axis_at, shards_of in cuts:
        draws = jnp.exp(jax.random.uniform(jax.random.fold_in(own, axis_at), (shards_of,), jnp.float32, smallest / len(cuts), high / len(cuts)))
        level = level * jnp.repeat(draws, dims[axis_at] // shards_of).reshape([-1 if axis == axis_at else 1 for axis in range(len(dims))])
    return level


def setup_inputs(seed: int = 0) -> dict:
    key_of = jax.random.split(jax.random.key(seed), 4)
    density = jnp.clip(jnp.exp(math.log(3.0) - 2.7080502 * jax.random.uniform(key_of[0], (NZ, NY, NX), jnp.float32) ** block_levels(key_of[0], (NZ, NY, NX), ((0, 8), (1, 16)), -0.2, 0.2)), 0.2, 3.0)
    occupancy = draw_occupancy(jax.random.fold_in(key_of[3], 71), 0)
    transfer = jnp.clip(jax.random.uniform(key_of[2], (2, 4), jnp.float32, -1.5, 1.5), -1.5, 1.5)
    return dict(density=density, occupancy=occupancy, transfer=transfer)


def voxels(window, transfer, ray_step):
    center = window[1, 1:-1, ..., 1:-1]
    grad_z = (window[2, 1:-1, ..., 1:-1] - window[0, 1:-1, ..., 1:-1]) * 0.5
    grad_y = (window[1, 2:, ..., 1:-1] - window[1, :-2, ..., 1:-1]) * 0.5
    grad_x = (window[1, 1:-1, ..., 2:] - window[1, 1:-1, ..., :-2]) * 0.5
    inv_norm = 1.0 / jnp.sqrt(grad_x * grad_x + grad_y * grad_y + grad_z * grad_z + 1.0)
    lighting = 0.3 + 0.7 * jnp.abs((0.48 * grad_z + 0.6 * grad_y + 0.64 * grad_x) * inv_norm)
    extinct = center * jax.nn.softplus(transfer[0, 3] * center + transfer[1, 3])
    opacity = 1.0 - jnp.exp(-ray_step * extinct)
    colors = jnp.stack([jax.nn.sigmoid(transfer[0, channel] * center + transfer[1, channel]) for channel in range(3)])
    return (opacity * lighting * colors, opacity)

def march(padded, transfer, ray_step):
    depth_count = padded.shape[0] - 2
    cell_shape = (padded.shape[1] - 2,) + padded.shape[2:-1] + (padded.shape[-1] - 2,)
    start_state = (jnp.zeros((3,) + cell_shape, jnp.float32), jnp.ones(cell_shape, jnp.float32))

    def advance(state_pair, depth_at):
        color_sum, transmit = state_pair
        window = lax.dynamic_slice_in_dim(padded, depth_at, 3, 0)
        shaded, opacity = voxels(window, transfer, ray_step)
        return ((color_sum + transmit * shaded, transmit * (1.0 - opacity)), None)
    (color_sum, transmit), _ = lax.scan(advance, start_state, jnp.arange(depth_count, dtype=jnp.int32))
    return (color_sum, transmit)

def reference(density, occupancy, transfer):
    block_flags = occupancy.astype(jnp.float32)
    blocks = density.reshape(NZ // BZ, BZ, NY // BY, BY, NX // CB, CB)
    masked = (blocks * block_flags[:, None, :, None, :, None]).reshape(NZ, NY, NX)
    padded = jnp.pad(masked, 1)
    ray_step = 2.0 / NZ

    def row_slab(slab_index):
        part_rows = lax.dynamic_slice_in_dim(padded, slab_index * BY, BY + 2, 1)
        color_sum, transmit = march(part_rows, transfer, ray_step)
        return jnp.concatenate([color_sum, (1.0 - transmit)[None]], 0)
    pieces = lax.map(row_slab, jnp.arange(NY // BY, dtype=jnp.int32))
    return jnp.transpose(pieces, (1, 0, 2, 3)).reshape(4, NY, NX)
```

```python
import functools

import jax
import jax.numpy as jnp
from jax import lax
from jax.experimental import pallas as pl
from jax.experimental.pallas import tpu as pltpu
from jax.sharding import PartitionSpec as P

MESH = pl.DeviceIdType.MESH
LOG2E = 1.4426950408889634
LANES = 128
PAD = 8
SLOTS = 12
CHUNKS = 8


def remote(src, dst, send_sem, recv_sem, **where):
    return pltpu.make_async_remote_copy(
        src_ref=src,
        dst_ref=dst,
        send_sem=send_sem,
        recv_sem=recv_sem,
        device_id=where,
        device_id_type=MESH,
    )


def blend(mine, theirs, mine_in_front):
    front = [jnp.where(mine_in_front, a, b) for a, b in zip(mine, theirs)]
    back = [jnp.where(mine_in_front, b, a) for a, b in zip(mine, theirs)]
    return [front[c] + front[3] * back[c] for c in range(3)] + [front[3] * back[3]]


def kernel(
    dims,
    occ,
    transfer,
    density,
    out,
    brick,
    z_recv,
    z_edge,
    flags,
    z_flags,
    y_send,
    y_recv,
    slots,
    keep1,
    send1,
    recv1,
    keep_a,
    send_a,
    recv_a,
    keep_b,
    send_b,
    recv_b,
    slot_block,
    left_of,
    right_of,
    slot_of,
    load_sem,
    z_sems,
    f_sems,
    y_sems,
    sems1,
    sems_a,
    sems_b,
):
    cells, rows, blocks, depth_n, rows_n = dims
    chunk_rows = rows // CHUNKS
    depth_at, row_at = lax.axis_index("depth"), lax.axis_index("rows")
    chip, core = depth_at // 2, depth_at % 2
    edge_chip = jnp.where(jnp.logical_or(chip == 0, chip == 3), 1, 0)
    sibling = depth_at + 1 - 2 * core
    pair_a = depth_at + 2 - 4 * (chip % 2)
    pair_b = (3 - chip) * 2 + core
    has_front, has_back = depth_at > 0, depth_at < depth_n - 1
    has_up, has_down = row_at > 0, row_at < rows_n - 1
    far = depth_at + 2 * core - 1
    has_far = jnp.logical_and(far >= 0, far < depth_n)

    loads = [
        pltpu.make_async_copy(
            density.at[:, :, pl.ds(LANES * b, LANES)],
            brick.at[b, :, pl.ds(PAD, rows), :],
            load_sem.at[b],
        )
        for b in range(blocks)
    ]
    for copy in loads:
        copy.start()

    barrier = pltpu.get_barrier_semaphore()

    def greet(**where):
        pl.semaphore_signal(barrier, inc=1, device_id=where, device_id_type=MESH)

    greet(depth=sibling)
    greet(depth=pair_a)
    greet(depth=pair_b)

    @pl.when(has_far)
    def _():
        greet(depth=far)

    @pl.when(has_up)
    def _():
        greet(rows=row_at - 1)

    @pl.when(has_down)
    def _():
        greet(rows=row_at + 1)

    peers = 3
    for condition in (has_far, has_up, has_down):
        peers = peers + jnp.where(condition, 1, 0)
    pl.semaphore_wait(barrier, peers)

    for b in range(blocks):
        flags[pl.ds(b, 1), :] = jnp.full((1, LANES), occ[0, 0, b], jnp.int32).astype(jnp.float32)

    def chunk_at(t):
        return lax.rem(t + 1, CHUNKS)

    def z_copy(side, c):
        span = pl.ds(pl.multiple_of(c * chunk_rows, chunk_rows), chunk_rows)
        return remote(
            density.at[cells - 1 if side == 0 else 0, span, :],
            z_recv.at[side, span, :],
            z_sems.at[0, side, c],
            z_sems.at[1, side, c],
            depth=depth_at + 1 if side == 0 else depth_at - 1,
        )

    def flag_copy(side):
        return remote(
            flags,
            z_flags.at[side],
            f_sems.at[0, side],
            f_sems.at[1, side],
            depth=depth_at + 1 if side == 0 else depth_at - 1,
        )

    def y_copy(side):
        return remote(
            y_send.at[side],
            y_recv.at[side],
            y_sems.at[0, side],
            y_sems.at[1, side],
            rows=row_at + 1 if side == 0 else row_at - 1,
        )

    z_sends, z_receives = (has_back, has_front), (has_front, has_back)
    y_sends, y_receives = (has_down, has_up), (has_up, has_down)

    for side in range(2):

        @pl.when(z_sends[side])
        def _(side=side):
            flag_copy(side).start()

    def start_halo(t, carry):
        for side in range(2):

            @pl.when(z_sends[side])
            def _(side=side):
                z_copy(side, chunk_at(t)).start()

        return carry

    lax.fori_loop(0, CHUNKS, start_halo, 0)

    occupied = [occ[0, 0, b] for b in range(blocks)]
    before, count = [], jnp.int32(0)
    for b in range(blocks):
        before.append(count)
        count = count + occupied[b]
    for s in range(SLOTS):
        found = jnp.int32(0)
        for b in range(1, blocks):
            hit = jnp.logical_and(occupied[b] == 1, before[b] == s)
            found = jnp.where(hit, b, found)
        slot_block[s] = found
    for b in range(blocks):
        slot_of[b] = jnp.where(occupied[b] == 1, before[b], SLOTS)
        left_of[b] = blocks if b == 0 else jnp.where(occupied[b - 1] == 1, b - 1, blocks)
        right_of[b] = (
            blocks if b == blocks - 1 else jnp.where(occupied[b + 1] == 1, b + 1, blocks)
        )

    def clear(z, carry):
        brick[blocks, z] = jnp.zeros(brick.shape[2:], jnp.float32)
        return carry

    lax.fori_loop(0, cells, clear, 0)
    for c in range(4):
        slots[c, SLOTS] = jnp.full((chunk_rows, LANES), float(c == 3), jnp.float32)
    for side in range(2):

        @pl.when(jnp.logical_not(z_receives[side]))
        def _(side=side):
            z_edge[side] = jnp.zeros(z_edge.shape[1:], jnp.float32)

    for copy in loads:
        copy.wait()

    def pack(b, carry):
        flag = flags[pl.ds(b, 1), :]
        for z in range(cells):
            y_send[0, b, pl.ds(z, 1), :] = brick[b, z, pl.ds(PAD + rows - 1, 1), :] * flag
            y_send[1, b, pl.ds(z, 1), :] = brick[b, z, pl.ds(PAD, 1), :] * flag
        return carry

    lax.fori_loop(0, blocks, pack, 0)
    for side in range(2):

        @pl.when(y_sends[side])
        def _(side=side):
            y_copy(side).start()

        @pl.when(z_receives[side])
        def _(side=side):
            flag_copy(side).wait_recv()

    halo_row = (PAD - 1, PAD + rows)

    def unpack():
        for side in range(2):

            @pl.when(y_receives[side])
            def _(side=side):
                y_copy(side).wait_recv()

                def one(b, carry):
                    for z in range(cells):
                        brick[b, z, pl.ds(halo_row[side], 1), :] = y_recv[side, b, pl.ds(z, 1), :]
                    return carry

                lax.fori_loop(0, blocks, one, 0)

            @pl.when(jnp.logical_not(y_receives[side]))
            def _(side=side):
                def one(b, carry):
                    for z in range(cells):
                        brick[b, z, pl.ds(halo_row[side], 1), :] = jnp.zeros(
                            (1, LANES), jnp.float32
                        )
                    return carry

                lax.fori_loop(0, blocks, one, 0)

    lane = lax.broadcasted_iota(jnp.int32, (chunk_rows, LANES), 1)
    first_lane, last_lane = lane == 0, lane == LANES - 1
    ext_slope, ext_offset = transfer[0, 3] * LOG2E, transfer[1, 3] * LOG2E
    step_scale = -2.0 / (cells * depth_n) * LOG2E
    channels = [(transfer[0, c] * 0.5, transfer[1, c] * 0.5) for c in range(3)]

    def march(s, first_row):
        b = slot_block[s]
        left, right = left_of[b], right_of[b]
        row = pl.multiple_of(PAD + first_row, 8)
        previous, center = z_edge[0, b], brick[b, 0, pl.ds(row, chunk_rows), :]
        transmit = jnp.ones((chunk_rows, LANES), jnp.float32)
        total = jnp.zeros((chunk_rows, LANES), jnp.float32)
        sums = [jnp.zeros((chunk_rows, LANES), jnp.float32) for _ in range(3)]
        for z in range(cells):
            following = (
                brick[b, z + 1, pl.ds(row, chunk_rows), :] if z + 1 < cells else z_edge[1, b]
            )
            diff_z = following - previous
            diff_y = (
                brick[b, z, pl.ds(row + 1, chunk_rows), :]
                - brick[b, z, pl.ds(row - 1, chunk_rows), :]
            )
            beside = brick[right, z, pl.ds(row, chunk_rows), :]
            after = pltpu.roll(jnp.where(first_lane, beside, center), LANES - 1, 1)
            beside = brick[left, z, pl.ds(row, chunk_rows), :]
            ahead = pltpu.roll(jnp.where(last_lane, beside, center), 1, 1)
            diff_x = after - ahead
            slope = jnp.abs(0.168 * diff_z + 0.21 * diff_y + 0.224 * diff_x)
            norm = diff_x * diff_x + diff_y * diff_y + (diff_z * diff_z + 4.0)
            lighting = 0.15 + slope * lax.rsqrt(norm)
            grown = 1.0 + jnp.exp2(ext_slope * center + ext_offset)
            kept = transmit * jnp.exp2((step_scale * center) * jnp.log(grown))
            weight = (transmit - kept) * lighting
            transmit = kept
            total = total + weight
            for c in range(3):
                slope_c, offset_c = channels[c]
                sums[c] = sums[c] + weight * jnp.tanh(slope_c * center + offset_c)
            previous, center = center, following
        for c in range(3):
            slots[c, s] = total + sums[c]
        slots[3, s] = transmit

    def copy1(c):
        return remote(
            send1.at[c], recv1.at[c], sems1.at[0, c], sems1.at[1, c], depth=sibling
        )

    def copy_a(c):
        return remote(
            send_a.at[c], recv_a.at[c], sems_a.at[0, c], sems_a.at[1, c], depth=pair_a
        )

    def copy_b(c):
        return remote(
            send_b.at[c], recv_b.at[c], sems_b.at[0, c], sems_b.at[1, c], depth=pair_b
        )

    def hand_over(c):
        for q in range(blocks // 2):
            theirs = slot_of[4 * (q // 2) + q % 2 + 2 * (1 - core)]
            mine = slot_of[4 * (q // 2) + q % 2 + 2 * core]
            for ch in range(4):
                send1[c, q, ch] = slots[ch, theirs]
        copy1(c).start()
        for q in range(blocks // 2):
            mine = slot_of[4 * (q // 2) + q % 2 + 2 * core]
            for ch in range(4):
                keep1[q, ch] = slots[ch, mine]

    def stage_a(c):
        copy1(c).wait_recv()

        def merged(q):
            return blend(
                [keep1[q, ch] for ch in range(4)],
                [recv1[c, q, ch] for ch in range(4)],
                core == 0,
            )

        for n in range(2):
            dest = n + n * 2 * (1 - edge_chip) + edge_chip
            for i in range(2):
                for ch, value in enumerate(merged(dest * 2 + i)):
                    send_a[c, n * 2 + i, ch] = value
        copy_a(c).start()
        for n in range(2):
            dest = n + n * 2 * edge_chip + (1 - edge_chip)
            for i in range(2):
                for ch, value in enumerate(merged(dest * 2 + i)):
                    keep_a[c, n * 2 + i, ch] = value

    def stage_b(c):
        copy_a(c).wait_recv()
        own = chip // 2

        def merged(p):
            return blend(
                [keep_a[c, p, ch] for ch in range(4)],
                [recv_a[c, p, ch] for ch in range(4)],
                chip % 2 == 0,
            )

        for i in range(2):
            for ch, value in enumerate(merged((1 - own) * 2 + i)):
                send_b[c, i, ch] = value
        copy_b(c).start()
        for i in range(2):
            for ch, value in enumerate(merged(own * 2 + i)):
                keep_b[c, i, ch] = value

    def finish(c):
        copy_b(c).wait_recv()
        span = pl.ds(pl.multiple_of(c * chunk_rows, chunk_rows), chunk_rows)
        for i in range(2):
            value = blend(
                [keep_b[c, i, ch] for ch in range(4)],
                [recv_b[c, i, ch] for ch in range(4)],
                chip < 2,
            )
            value[3] = 1.0 - value[3]
            for ch in range(4):
                out[ch, span, pl.ds(i * LANES, LANES)] = value[ch]

    lag_a, lag_b, lag_f = 1, 2, 3

    def one_chunk(t, carry):
        c = chunk_at(t)
        first_row = pl.multiple_of(c * chunk_rows, chunk_rows)

        @pl.when(t == CHUNKS - 2)
        def _():
            unpack()

        for side in range(2):

            @pl.when(z_receives[side])
            def _(side=side):
                z_copy(side, c).wait_recv()
                for b in range(blocks):
                    layer = z_recv[
                        side, pl.ds(first_row, chunk_rows), pl.ds(b * LANES, LANES)
                    ]
                    z_edge[side, b] = layer * z_flags[side, pl.ds(b, 1), :]

        def one_slot(s, inner):
            march(s, first_row)

            @pl.when(jnp.logical_and(s == 3, t >= lag_a))
            def _():
                stage_a(chunk_at(t - lag_a))

            @pl.when(jnp.logical_and(s == 7, t >= lag_b))
            def _():
                stage_b(chunk_at(t - lag_b))

            @pl.when(jnp.logical_and(s == 9, t >= lag_f))
            def _():
                finish(chunk_at(t - lag_f))

            return inner

        lax.fori_loop(0, SLOTS, one_slot, 0)
        hand_over(c)
        return carry

    lax.fori_loop(0, CHUNKS, one_chunk, 0)

    def tail(t, carry):
        @pl.when(t - lag_a < CHUNKS)
        def _():
            stage_a(chunk_at(t - lag_a))

        @pl.when(t - lag_b < CHUNKS)
        def _():
            stage_b(chunk_at(t - lag_b))

        finish(chunk_at(t - lag_f))
        return carry

    lax.fori_loop(CHUNKS, CHUNKS + lag_f, tail, 0)

    for side in range(2):

        @pl.when(z_sends[side])
        def _(side=side):
            flag_copy(side).wait_send()

        @pl.when(y_sends[side])
        def _(side=side):
            y_copy(side).wait_send()

    def drain(c, carry):
        for side in range(2):

            @pl.when(z_sends[side])
            def _(side=side):
                z_copy(side, c).wait_send()

        copy1(c).wait_send()
        copy_a(c).wait_send()
        copy_b(c).wait_send()
        return carry

    lax.fori_loop(0, CHUNKS, drain, 0)


def solution(mesh):
    depth_n, rows_n = mesh.shape["depth"], mesh.shape["rows"]

    def shards(density, occupancy, transfer):
        cells, rows, columns = density.shape
        blocks = columns // LANES
        chunk_rows = rows // CHUNKS
        half, quarter, eighth = blocks // 2, blocks // 4, blocks // 8
        f32 = jnp.float32
        tile = (chunk_rows, LANES)
        dma = pltpu.SemaphoreType.DMA
        return pl.pallas_call(
            functools.partial(kernel, (cells, rows, blocks, depth_n, rows_n)),
            out_shape=jax.ShapeDtypeStruct((4, rows, columns // depth_n), f32),
            in_specs=[
                pl.BlockSpec(memory_space=pltpu.SMEM),
                pl.BlockSpec(memory_space=pltpu.SMEM),
                pl.BlockSpec(memory_space=pl.ANY),
            ],
            out_specs=pl.BlockSpec(memory_space=pltpu.VMEM),
            scratch_shapes=[
                pltpu.VMEM((blocks + 1, cells, rows + 2 * PAD, LANES), f32),
                pltpu.VMEM((2, rows, columns), f32),
                pltpu.VMEM((2, blocks) + tile, f32),
                pltpu.VMEM((blocks, LANES), f32),
                pltpu.VMEM((2, blocks, LANES), f32),
                pltpu.VMEM((2, blocks, cells, LANES), f32),
                pltpu.VMEM((2, blocks, cells, LANES), f32),
                pltpu.VMEM((4, SLOTS + 1) + tile, f32),
                pltpu.VMEM((half, 4) + tile, f32),
                pltpu.VMEM((CHUNKS, half, 4) + tile, f32),
                pltpu.VMEM((CHUNKS, half, 4) + tile, f32),
                pltpu.VMEM((CHUNKS, quarter, 4) + tile, f32),
                pltpu.VMEM((CHUNKS, quarter, 4) + tile, f32),
                pltpu.VMEM((CHUNKS, quarter, 4) + tile, f32),
                pltpu.VMEM((CHUNKS, eighth, 4) + tile, f32),
                pltpu.VMEM((CHUNKS, eighth, 4) + tile, f32),
                pltpu.VMEM((CHUNKS, eighth, 4) + tile, f32),
                pltpu.SMEM((SLOTS,), jnp.int32),
                pltpu.SMEM((blocks,), jnp.int32),
                pltpu.SMEM((blocks,), jnp.int32),
                pltpu.SMEM((blocks,), jnp.int32),
                dma((blocks,)),
                dma((2, 2, CHUNKS)),
                dma((2, 2)),
                dma((2, 2)),
                dma((2, CHUNKS)),
                dma((2, CHUNKS)),
                dma((2, CHUNKS)),
            ],
            compiler_params=pltpu.CompilerParams(
                collective_id=0,
                has_side_effects=True,
                vmem_limit_bytes=56 * 2**20,
            ),
        )(occupancy, transfer, density)

    return jax.shard_map(
        shards,
        mesh=mesh,
        in_specs=(P("depth", "rows", None), P("depth", "rows", None), P()),
        out_specs=P(None, "rows", "depth"),
        check_vma=False,
    )
```

```python
import functools

import jax
import jax.numpy as jnp
from jax import lax
from jax.experimental import pallas as pl
from jax.experimental.pallas import tpu as pltpu
from jax.sharding import PartitionSpec as P

MESH = pl.DeviceIdType.MESH
LOG2E = 1.4426950408889634
LANES = 128
PAD = 8
SLOTS = 12
CHUNKS = 8
AHEAD = 2
GROUP = 2
LIGHT_SCALE = 0.224
LIGHT_FLOOR = 0.15 / LIGHT_SCALE


def remote(src, dst, send_sem, recv_sem, **where):
    return pltpu.make_async_remote_copy(
        src_ref=src,
        dst_ref=dst,
        send_sem=send_sem,
        recv_sem=recv_sem,
        device_id=where,
        device_id_type=MESH,
    )


def blend(mine, theirs, mine_in_front):
    front = [jnp.where(mine_in_front, a, b) for a, b in zip(mine, theirs)]
    back = [jnp.where(mine_in_front, b, a) for a, b in zip(mine, theirs)]
    return [front[c] + front[3] * back[c] for c in range(3)] + [front[3] * back[3]]


def kernel(
    dims,
    occ,
    transfer,
    density,
    out,
    brick,
    window,
    z_recv,
    z_edge,
    flags,
    z_flags,
    y_send,
    y_recv,
    slots,
    keep1,
    send1,
    recv1,
    send2,
    recv2,
    slot_block,
    left_of,
    right_of,
    slot_of,
    load_sem,
    window_sem,
    z_sems,
    f_sems,
    y_sems,
    sems1,
    sems2,
):
    cells, rows, blocks, depth_n, rows_n = dims
    chunk_rows = rows // CHUNKS
    depth_at, row_at = lax.axis_index("depth"), lax.axis_index("rows")
    chip, core = depth_at // 2, depth_at % 2
    sibling = depth_at + 1 - 2 * core
    has_front, has_back = depth_at > 0, depth_at < depth_n - 1
    has_up, has_down = row_at > 0, row_at < rows_n - 1
    far = depth_at + 2 * core - 1
    has_far = jnp.logical_and(far >= 0, far < depth_n)

    window_row = chunk_rows - PAD
    window_loads = [
        pltpu.make_async_copy(
            density.at[:, pl.ds(window_row, window.shape[2]), pl.ds(LANES * b, LANES)],
            window.at[b],
            window_sem.at[b],
        )
        for b in range(blocks)
    ]
    loads = [
        pltpu.make_async_copy(
            density.at[:, :, pl.ds(LANES * b, LANES)],
            brick.at[b, :, pl.ds(PAD, rows), :],
            load_sem.at[b],
        )
        for b in range(blocks)
    ]
    for copy in window_loads + loads:
        copy.start()

    barrier = pltpu.get_barrier_semaphore()

    def greet(**where):
        pl.semaphore_signal(barrier, inc=1, device_id=where, device_id_type=MESH)

    greet(depth=sibling)
    for offset in range(1, 4):
        greet(depth=lax.rem(depth_at + 2 * offset, depth_n))

    @pl.when(has_far)
    def _():
        greet(depth=far)

    @pl.when(has_up)
    def _():
        greet(rows=row_at - 1)

    @pl.when(has_down)
    def _():
        greet(rows=row_at + 1)

    for b in range(blocks):
        flags[pl.ds(b, 1), :] = jnp.full((1, LANES), occ[0, 0, b], jnp.int32).astype(jnp.float32)

    def chunk_at(t):
        return lax.rem(t + 1, CHUNKS)

    def z_copy(side, c):
        span = pl.ds(pl.multiple_of(c * chunk_rows, chunk_rows), chunk_rows)
        return remote(
            density.at[cells - 1 if side == 0 else 0, span, :],
            z_recv.at[side, span, :],
            z_sems.at[0, side, c],
            z_sems.at[1, side, c],
            depth=depth_at + 1 if side == 0 else depth_at - 1,
        )

    def flag_copy(side):
        return remote(
            flags,
            z_flags.at[side],
            f_sems.at[0, side],
            f_sems.at[1, side],
            depth=depth_at + 1 if side == 0 else depth_at - 1,
        )

    def y_copy(side):
        return remote(
            y_send.at[side],
            y_recv.at[side],
            y_sems.at[0, side],
            y_sems.at[1, side],
            rows=row_at + 1 if side == 0 else row_at - 1,
        )

    z_sends, z_receives = (has_back, has_front), (has_front, has_back)
    y_sends, y_receives = (has_down, has_up), (has_up, has_down)

    occupied = [occ[0, 0, b] for b in range(blocks)]
    before, count = [], jnp.int32(0)
    for b in range(blocks):
        before.append(count)
        count = count + occupied[b]
    for s in range(SLOTS):
        found = jnp.int32(0)
        for b in range(1, blocks):
            hit = jnp.logical_and(occupied[b] == 1, before[b] == s)
            found = jnp.where(hit, b, found)
        slot_block[s] = found
    for b in range(blocks):
        slot_of[b] = jnp.where(occupied[b] == 1, before[b], SLOTS)
        left_of[b] = blocks if b == 0 else jnp.where(occupied[b - 1] == 1, b - 1, blocks)
        right_of[b] = (
            blocks if b == blocks - 1 else jnp.where(occupied[b + 1] == 1, b + 1, blocks)
        )

    def clear(z, carry):
        brick[blocks, z] = jnp.zeros(brick.shape[2:], jnp.float32)
        window[blocks, z] = jnp.zeros(window.shape[2:], jnp.float32)
        return carry

    lax.fori_loop(0, cells, clear, 0)
    for r in range(AHEAD + 1):
        for c in range(4):
            slots[r, c, SLOTS] = jnp.full((chunk_rows, LANES), float(c == 3), jnp.float32)
    for side in range(2):

        @pl.when(jnp.logical_not(z_receives[side]))
        def _(side=side):
            z_edge[side] = jnp.zeros(z_edge.shape[1:], jnp.float32)

    halo_row = (PAD - 1, PAD + rows)

    def unpack():
        for side in range(2):

            @pl.when(y_receives[side])
            def _(side=side):
                y_copy(side).wait_recv()

                def one(b, carry):
                    for z in range(cells):
                        brick[b, z, pl.ds(halo_row[side], 1), :] = y_recv[side, b, pl.ds(z, 1), :]
                    return carry

                lax.fori_loop(0, blocks, one, 0)

            @pl.when(jnp.logical_not(y_receives[side]))
            def _(side=side):
                def one(b, carry):
                    for z in range(cells):
                        brick[b, z, pl.ds(halo_row[side], 1), :] = jnp.zeros(
                            (1, LANES), jnp.float32
                        )
                    return carry

                lax.fori_loop(0, blocks, one, 0)

    lane = lax.broadcasted_iota(jnp.int32, (chunk_rows, LANES), 1)
    first_lane, last_lane = lane == 0, lane == LANES - 1
    ext_slope, ext_offset = transfer[0, 3] * LOG2E, transfer[1, 3] * LOG2E
    step_scale = -2.0 / (cells * depth_n) * LOG2E
    channels = [(transfer[0, c] * 0.5, transfer[1, c] * 0.5) for c in range(3)]

    def shade(center, diff_z, diff_y, beside_left, beside_right, transmit):
        after = pltpu.roll(jnp.where(first_lane, beside_right, center), LANES - 1, 1)
        ahead = pltpu.roll(jnp.where(last_lane, beside_left, center), 1, 1)
        diff_x = after - ahead
        slope = jnp.abs(0.75 * diff_z + 0.9375 * diff_y + diff_x)
        norm = diff_x * diff_x + diff_y * diff_y + (diff_z * diff_z + 4.0)
        lighting = LIGHT_FLOOR + slope * lax.rsqrt(norm)
        grown = 1.0 + jnp.exp2(ext_slope * center + ext_offset)
        factor = jnp.exp2((step_scale * center) * jnp.log(grown))
        kept = factor if transmit is None else transmit * factor
        weight = ((1.0 if transmit is None else transmit) - kept) * lighting
        return kept, weight, [jnp.tanh(slope_c * center + offset_c) for slope_c, offset_c in channels]

    def cell_rows(ref, b, z, row):
        return ref[b, z, pl.ds(row, chunk_rows), :]

    def layer(ref, b, z, row, center, diff_z, transmit):
        diff_y = cell_rows(ref, b, z, row + 1) - cell_rows(ref, b, z, row - 1)
        return shade(
            center,
            diff_z,
            diff_y,
            cell_rows(ref, left_of[b], z, row),
            cell_rows(ref, right_of[b], z, row),
            transmit,
        )

    def march(ref, ring, first_slot, row):
        group = range(GROUP)
        block = [slot_block[first_slot + g] for g in group]
        previous = [cell_rows(ref, block[g], 0, row) for g in group]
        center = [cell_rows(ref, block[g], 1, row) for g in group]
        transmit, total, sums = [None] * GROUP, [None] * GROUP, [None] * GROUP
        for z in range(1, cells - 1):
            for g in group:
                following = cell_rows(ref, block[g], z + 1, row)
                kept, weight, factors = layer(
                    ref, block[g], z, row, center[g], following - previous[g], transmit[g]
                )
                products = [weight * f for f in factors]
                if total[g] is None:
                    total[g], sums[g] = weight, products
                else:
                    total[g] = total[g] + weight
                    sums[g] = [a + b for a, b in zip(sums[g], products)]
                transmit[g] = kept
                previous[g], center[g] = center[g], following
        for g in group:
            for c in range(3):
                slots[ring, c, first_slot + g] = LIGHT_SCALE * (total[g] + sums[g][c])
            slots[ring, 3, first_slot + g] = transmit[g]

    def ends(ring, first_slot, row):
        for g in range(GROUP):
            s = first_slot + g
            b = slot_block[s]
            color = [slots[ring, c, s] for c in range(3)]
            last = cells - 1
            center = cell_rows(brick, b, 0, row)
            diff_z = cell_rows(brick, b, 1, row) - z_edge[0, b]
            kept, weight, factors = layer(brick, b, 0, row, center, diff_z, None)
            weight = weight * LIGHT_SCALE
            color = [(weight + weight * f) + kept * c for f, c in zip(factors, color)]
            transmit = kept * slots[ring, 3, s]
            center = cell_rows(brick, b, last, row)
            diff_z = z_edge[1, b] - cell_rows(brick, b, last - 1, row)
            kept, weight, factors = layer(brick, b, last, row, center, diff_z, transmit)
            weight = weight * LIGHT_SCALE
            for c in range(3):
                slots[ring, c, s] = color[c] + (weight + weight * factors[c])
            slots[ring, 3, s] = kept

    def copy1(c):
        return remote(
            send1.at[c], recv1.at[c], sems1.at[0, c], sems1.at[1, c], depth=sibling
        )

    def copy2(c, offset):
        dest = lax.rem(chip + offset, 4)
        return remote(
            send2.at[c, dest],
            recv2.at[c, offset],
            sems2.at[0, offset - 1, c],
            sems2.at[1, offset - 1, c],
            depth=2 * dest + core,
        )

    def hand_over(c, ring):
        for q in range(blocks // 2):
            theirs = slot_of[4 * (q // 2) + q % 2 + 2 * (1 - core)]
            for ch in range(4):
                send1[c, q, ch] = slots[ring, ch, theirs]
        copy1(c).start()
        for q in range(blocks // 2):
            mine = slot_of[4 * (q // 2) + q % 2 + 2 * core]
            for ch in range(4):
                keep1[c, q, ch] = slots[ring, ch, mine]

    def merge(c):
        copy1(c).wait_recv()

        def merged(q):
            return blend(
                [keep1[c, q, ch] for ch in range(4)],
                [recv1[c, q, ch] for ch in range(4)],
                core == 0,
            )

        for offset in (2, 1, 3):
            dest = lax.rem(chip + offset, 4)
            for i in range(2):
                for ch, value in enumerate(merged(2 * dest + i)):
                    send2[c, dest, i, ch] = value
            copy2(c, offset).start()
        for i in range(2):
            for ch, value in enumerate(merged(2 * chip + i)):
                recv2[c, 0, i, ch] = value

    def finish(t, carry):
        c = chunk_at(t)
        for offset in range(1, 4):
            copy2(c, offset).wait_recv()
        span = pl.ds(pl.multiple_of(c * chunk_rows, chunk_rows), chunk_rows)
        for i in range(2):
            value = None
            for source in (3, 2, 1, 0):
                offset = lax.rem(chip - source + 4, 4)
                part = [recv2[c, offset, i, ch] for ch in range(4)]
                if value is None:
                    value = part
                else:
                    value = [part[k] + part[3] * value[k] for k in range(3)] + [part[3] * value[3]]
            value[3] = 1.0 - value[3]
            for ch in range(4):
                out[ch, span, pl.ds(i * LANES, LANES)] = value[ch]
        return carry

    def march_window(t):
        def one(s, carry):
            march(window, t, s * GROUP, PAD + t * chunk_rows)
            return carry

        lax.fori_loop(0, SLOTS // GROUP, one, 0)

    for copy in window_loads:
        copy.wait()
    march_window(0)
    peers = 4
    for condition in (has_far, has_up, has_down):
        peers = peers + jnp.where(condition, 1, 0)
    pl.semaphore_wait(barrier, peers)

    for side in range(2):

        @pl.when(z_sends[side])
        def _(side=side):
            flag_copy(side).start()

    def start_halo(t, carry):
        for side in range(2):

            @pl.when(z_sends[side])
            def _(side=side):
                z_copy(side, chunk_at(t)).start()

        return carry

    lax.fori_loop(0, CHUNKS, start_halo, 0)

    march_window(1)

    for copy in loads:
        copy.wait()

    def pack(b, carry):
        flag = flags[pl.ds(b, 1), :]
        for z in range(cells):
            y_send[0, b, pl.ds(z, 1), :] = brick[b, z, pl.ds(PAD + rows - 1, 1), :] * flag
            y_send[1, b, pl.ds(z, 1), :] = brick[b, z, pl.ds(PAD, 1), :] * flag
        return carry

    lax.fori_loop(0, blocks, pack, 0)
    for side in range(2):

        @pl.when(y_sends[side])
        def _(side=side):
            y_copy(side).start()

        @pl.when(z_receives[side])
        def _(side=side):
            flag_copy(side).wait_recv()

    def one_chunk(t, carry):
        c = chunk_at(t)
        first_row = pl.multiple_of(c * chunk_rows, chunk_rows)
        for side in range(2):

            @pl.when(z_receives[side])
            def _(side=side):
                z_copy(side, c).wait_recv()
                for b in range(blocks):
                    edge = z_recv[side, pl.ds(first_row, chunk_rows), pl.ds(b * LANES, LANES)]
                    z_edge[side, b] = edge * z_flags[side, pl.ds(b, 1), :]

        ring = lax.rem(t, AHEAD + 1)
        row = pl.multiple_of(PAD + first_row, 8)

        def one_end(s, inner):
            ends(ring, s * GROUP, row)
            return inner

        lax.fori_loop(0, SLOTS // GROUP, one_end, 0)
        hand_over(c, ring)

        @pl.when(t == CHUNKS - 2 - AHEAD)
        def _():
            unpack()

        @pl.when(t + AHEAD < CHUNKS)
        def _():
            later_ring = lax.rem(t + AHEAD, AHEAD + 1)
            later_row = pl.multiple_of(PAD + chunk_at(t + AHEAD) * chunk_rows, 8)

            def one_slot(s, inner):
                march(brick, later_ring, s * GROUP, later_row)

                @pl.when(s == SLOTS // GROUP - 2)
                def _():
                    merge(c)

                return inner

            lax.fori_loop(0, SLOTS // GROUP, one_slot, 0)

        return carry

    lax.fori_loop(0, CHUNKS, one_chunk, 0)
    for t in range(CHUNKS - AHEAD, CHUNKS):
        merge(chunk_at(t))
    lax.fori_loop(0, CHUNKS, finish, 0)

    for side in range(2):

        @pl.when(z_sends[side])
        def _(side=side):
            flag_copy(side).wait_send()

        @pl.when(y_sends[side])
        def _(side=side):
            y_copy(side).wait_send()

    def drain(c, carry):
        for side in range(2):

            @pl.when(z_sends[side])
            def _(side=side):
                z_copy(side, c).wait_send()

        copy1(c).wait_send()
        for offset in range(1, 4):
            copy2(c, offset).wait_send()
        return carry

    lax.fori_loop(0, CHUNKS, drain, 0)


def solution(mesh):
    depth_n, rows_n = mesh.shape["depth"], mesh.shape["rows"]

    def shards(density, occupancy, transfer):
        cells, rows, columns = density.shape
        blocks = columns // LANES
        chunk_rows = rows // CHUNKS
        half = blocks // 2
        f32 = jnp.float32
        tile = (chunk_rows, LANES)
        dma = pltpu.SemaphoreType.DMA
        return pl.pallas_call(
            functools.partial(kernel, (cells, rows, blocks, depth_n, rows_n)),
            out_shape=jax.ShapeDtypeStruct((4, rows, columns // depth_n), f32),
            in_specs=[
                pl.BlockSpec(memory_space=pltpu.SMEM),
                pl.BlockSpec(memory_space=pltpu.SMEM),
                pl.BlockSpec(memory_space=pl.ANY),
            ],
            out_specs=pl.BlockSpec(memory_space=pltpu.VMEM),
            scratch_shapes=[
                pltpu.VMEM((blocks + 1, cells, rows + 2 * PAD, LANES), f32),
                pltpu.VMEM((blocks + 1, cells, AHEAD * chunk_rows + 2 * PAD, LANES), f32),
                pltpu.VMEM((2, rows, columns), f32),
                pltpu.VMEM((2, blocks) + tile, f32),
                pltpu.VMEM((blocks, LANES), f32),
                pltpu.VMEM((2, blocks, LANES), f32),
                pltpu.VMEM((2, blocks, cells, LANES), f32),
                pltpu.VMEM((2, blocks, cells, LANES), f32),
                pltpu.VMEM((AHEAD + 1, 4, SLOTS + 1) + tile, f32),
                pltpu.VMEM((CHUNKS, half, 4) + tile, f32),
                pltpu.VMEM((CHUNKS, half, 4) + tile, f32),
                pltpu.VMEM((CHUNKS, half, 4) + tile, f32),
                pltpu.VMEM((CHUNKS, 4, 2, 4) + tile, f32),
                pltpu.VMEM((CHUNKS, 4, 2, 4) + tile, f32),
                pltpu.SMEM((SLOTS,), jnp.int32),
                pltpu.SMEM((blocks,), jnp.int32),
                pltpu.SMEM((blocks,), jnp.int32),
                pltpu.SMEM((blocks,), jnp.int32),
                dma((blocks,)),
                dma((blocks,)),
                dma((2, 2, CHUNKS)),
                dma((2, 2)),
                dma((2, 2)),
                dma((2, CHUNKS)),
                dma((2, 3, CHUNKS)),
            ],
            compiler_params=pltpu.CompilerParams(
                collective_id=0,
                has_side_effects=True,
                vmem_limit_bytes=60 * 2**20,
            ),
        )(occupancy, transfer, density)

    return jax.shard_map(
        shards,
        mesh=mesh,
        in_specs=(P("depth", "rows", None), P("depth", "rows", None), P()),
        out_specs=P(None, "rows", "depth"),
        check_vma=False,
    )
```

```python
import functools

import jax
import jax.numpy as jnp
from jax import lax
from jax.experimental import pallas as pl
from jax.experimental.pallas import tpu as pltpu
from jax.sharding import PartitionSpec as P

MESH = pl.DeviceIdType.MESH
LOG2E = 1.4426950408889634
LANES = 128
PAD = 8
SLOTS = 12
CHUNKS = 8
AHEAD = 2
GROUP = 4
LIGHT_SCALE = 0.224
LIGHT_FLOOR = 0.15 / LIGHT_SCALE


def remote(src, dst, send_sem, recv_sem, **where):
    return pltpu.make_async_remote_copy(
        src_ref=src,
        dst_ref=dst,
        send_sem=send_sem,
        recv_sem=recv_sem,
        device_id=where,
        device_id_type=MESH,
    )


def blend(mine, theirs, mine_in_front):
    front = [jnp.where(mine_in_front, a, b) for a, b in zip(mine, theirs)]
    back = [jnp.where(mine_in_front, b, a) for a, b in zip(mine, theirs)]
    return [front[c] + front[3] * back[c] for c in range(3)] + [front[3] * back[3]]


def kernel(
    dims,
    occ,
    transfer,
    density,
    out,
    brick,
    window,
    z_recv,
    z_edge,
    flags,
    z_flags,
    y_send,
    y_recv,
    slots,
    keep1,
    send1,
    recv1,
    send2,
    recv2,
    slot_block,
    left_of,
    right_of,
    slot_of,
    load_sem,
    window_sem,
    z_sems,
    f_sems,
    y_sems,
    sems1,
    sems2,
):
    cells, rows, blocks, depth_n, rows_n = dims
    chunk_rows = rows // CHUNKS
    depth_at, row_at = lax.axis_index("depth"), lax.axis_index("rows")
    chip, core = depth_at // 2, depth_at % 2
    sibling = depth_at + 1 - 2 * core
    has_front, has_back = depth_at > 0, depth_at < depth_n - 1
    has_up, has_down = row_at > 0, row_at < rows_n - 1
    far = depth_at + 2 * core - 1
    has_far = jnp.logical_and(far >= 0, far < depth_n)

    barrier = pltpu.get_barrier_semaphore()

    def greet(**where):
        pl.semaphore_signal(barrier, inc=1, device_id=where, device_id_type=MESH)

    greet(depth=sibling)
    for offset in range(1, 4):
        greet(depth=lax.rem(depth_at + 2 * offset, depth_n))

    @pl.when(has_far)
    def _():
        greet(depth=far)

    @pl.when(has_up)
    def _():
        greet(rows=row_at - 1)

    @pl.when(has_down)
    def _():
        greet(rows=row_at + 1)

    window_row = chunk_rows - PAD
    window_loads = [
        pltpu.make_async_copy(
            density.at[:, pl.ds(window_row, window.shape[2]), pl.ds(LANES * b, LANES)],
            window.at[b],
            window_sem.at[b],
        )
        for b in range(blocks)
    ]
    loads = [
        pltpu.make_async_copy(
            density.at[:, :, pl.ds(LANES * b, LANES)],
            brick.at[b, :, pl.ds(PAD, rows), :],
            load_sem.at[b],
        )
        for b in range(blocks)
    ]
    for copy in window_loads:
        copy.start()

    for b in range(blocks):
        flags[pl.ds(b, 1), :] = jnp.full((1, LANES), occ[0, 0, b], jnp.int32).astype(jnp.float32)

    def chunk_at(t):
        return lax.rem(t + 1, CHUNKS)

    def z_copy(side, c):
        span = pl.ds(pl.multiple_of(c * chunk_rows, chunk_rows), chunk_rows)
        return remote(
            density.at[cells - 1 if side == 0 else 0, span, :],
            z_recv.at[side, span, :],
            z_sems.at[0, side, c],
            z_sems.at[1, side, c],
            depth=depth_at + 1 if side == 0 else depth_at - 1,
        )

    def flag_copy(side):
        return remote(
            flags,
            z_flags.at[side],
            f_sems.at[0, side],
            f_sems.at[1, side],
            depth=depth_at + 1 if side == 0 else depth_at - 1,
        )

    def y_copy(side):
        return remote(
            y_send.at[side],
            y_recv.at[side],
            y_sems.at[0, side],
            y_sems.at[1, side],
            rows=row_at + 1 if side == 0 else row_at - 1,
        )

    z_sends, z_receives = (has_back, has_front), (has_front, has_back)
    y_sends, y_receives = (has_down, has_up), (has_up, has_down)

    occupied = [occ[0, 0, b] for b in range(blocks)]
    before, count = [], jnp.int32(0)
    for b in range(blocks):
        before.append(count)
        count = count + occupied[b]
    for s in range(SLOTS):
        found = jnp.int32(0)
        for b in range(1, blocks):
            hit = jnp.logical_and(occupied[b] == 1, before[b] == s)
            found = jnp.where(hit, b, found)
        slot_block[s] = found
    for b in range(blocks):
        slot_of[b] = jnp.where(occupied[b] == 1, before[b], SLOTS)
        left_of[b] = blocks if b == 0 else jnp.where(occupied[b - 1] == 1, b - 1, blocks)
        right_of[b] = (
            blocks if b == blocks - 1 else jnp.where(occupied[b + 1] == 1, b + 1, blocks)
        )

    def clear(z, carry):
        brick[blocks, z] = jnp.zeros(brick.shape[2:], jnp.float32)
        window[blocks, z] = jnp.zeros(window.shape[2:], jnp.float32)
        return carry

    lax.fori_loop(0, cells, clear, 0)
    for r in range(AHEAD + 1):
        for c in range(4):
            slots[r, c, SLOTS] = jnp.full((chunk_rows, LANES), float(c == 3), jnp.float32)
    for side in range(2):

        @pl.when(jnp.logical_not(z_receives[side]))
        def _(side=side):
            z_edge[side] = jnp.zeros(z_edge.shape[1:], jnp.float32)

    halo_row = (PAD - 1, PAD + rows)

    def unpack():
        for side in range(2):

            @pl.when(y_receives[side])
            def _(side=side):
                y_copy(side).wait_recv()

                def one(b, carry):
                    for z in range(cells):
                        brick[b, z, pl.ds(halo_row[side], 1), :] = y_recv[side, b, pl.ds(z, 1), :]
                    return carry

                lax.fori_loop(0, blocks, one, 0)

            @pl.when(jnp.logical_not(y_receives[side]))
            def _(side=side):
                def one(b, carry):
                    for z in range(cells):
                        brick[b, z, pl.ds(halo_row[side], 1), :] = jnp.zeros(
                            (1, LANES), jnp.float32
                        )
                    return carry

                lax.fori_loop(0, blocks, one, 0)

    lane = lax.broadcasted_iota(jnp.int32, (chunk_rows, LANES), 1)
    first_lane, last_lane = lane == 0, lane == LANES - 1
    ext_slope, ext_offset = transfer[0, 3] * LOG2E, transfer[1, 3] * LOG2E
    step_scale = -2.0 / (cells * depth_n) * LOG2E
    channels = [(transfer[0, c] * 0.5, transfer[1, c] * 0.5) for c in range(3)]

    def shade(center, diff_z, diff_y, beside_left, beside_right, transmit):
        after = pltpu.roll(jnp.where(first_lane, beside_right, center), LANES - 1, 1)
        ahead = pltpu.roll(jnp.where(last_lane, beside_left, center), 1, 1)
        diff_x = after - ahead
        slope = jnp.abs(0.75 * diff_z + 0.9375 * diff_y + diff_x)
        norm = diff_x * diff_x + diff_y * diff_y + (diff_z * diff_z + 4.0)
        lighting = LIGHT_FLOOR + slope * lax.rsqrt(norm)
        grown = 1.0 + jnp.exp2(ext_slope * center + ext_offset)
        factor = jnp.exp2((step_scale * center) * jnp.log(grown))
        kept = factor if transmit is None else transmit * factor
        weight = ((1.0 if transmit is None else transmit) - kept) * lighting
        return kept, weight, [jnp.tanh(slope_c * center + offset_c) for slope_c, offset_c in channels]

    def cell_rows(ref, b, z, row):
        return ref[b, z, pl.ds(row, chunk_rows), :]

    def layer(ref, b, z, row, center, diff_z, transmit):
        diff_y = cell_rows(ref, b, z, row + 1) - cell_rows(ref, b, z, row - 1)
        return shade(
            center,
            diff_z,
            diff_y,
            cell_rows(ref, left_of[b], z, row),
            cell_rows(ref, right_of[b], z, row),
            transmit,
        )

    def march(ref, ring, first_slot, row):
        group = range(GROUP)
        block = [slot_block[first_slot + g] for g in group]
        previous = [cell_rows(ref, block[g], 0, row) for g in group]
        center = [cell_rows(ref, block[g], 1, row) for g in group]
        transmit, total, sums = [None] * GROUP, [None] * GROUP, [None] * GROUP
        for z in range(1, cells - 1):
            for g in group:
                following = cell_rows(ref, block[g], z + 1, row)
                kept, weight, factors = layer(
                    ref, block[g], z, row, center[g], following - previous[g], transmit[g]
                )
                products = [weight * f for f in factors]
                if total[g] is None:
                    total[g], sums[g] = weight, products
                else:
                    total[g] = total[g] + weight
                    sums[g] = [a + b for a, b in zip(sums[g], products)]
                transmit[g] = kept
                previous[g], center[g] = center[g], following
        for g in group:
            for c in range(3):
                slots[ring, c, first_slot + g] = LIGHT_SCALE * (total[g] + sums[g][c])
            slots[ring, 3, first_slot + g] = transmit[g]

    def ends(ring, first_slot, row):
        for g in range(GROUP):
            s = first_slot + g
            b = slot_block[s]
            color = [slots[ring, c, s] for c in range(3)]
            last = cells - 1
            center = cell_rows(brick, b, 0, row)
            diff_z = cell_rows(brick, b, 1, row) - z_edge[0, b]
            kept, weight, factors = layer(brick, b, 0, row, center, diff_z, None)
            weight = weight * LIGHT_SCALE
            color = [(weight + weight * f) + kept * c for f, c in zip(factors, color)]
            transmit = kept * slots[ring, 3, s]
            center = cell_rows(brick, b, last, row)
            diff_z = z_edge[1, b] - cell_rows(brick, b, last - 1, row)
            kept, weight, factors = layer(brick, b, last, row, center, diff_z, transmit)
            weight = weight * LIGHT_SCALE
            for c in range(3):
                slots[ring, c, s] = color[c] + (weight + weight * factors[c])
            slots[ring, 3, s] = kept

    def copy1(c):
        return remote(
            send1.at[c], recv1.at[c], sems1.at[0, c], sems1.at[1, c], depth=sibling
        )

    def copy2(c, offset):
        dest = lax.rem(chip + offset, 4)
        return remote(
            send2.at[c, dest],
            recv2.at[c, offset],
            sems2.at[0, offset - 1, c],
            sems2.at[1, offset - 1, c],
            depth=2 * dest + core,
        )

    def hand_over(c, ring):
        for q in range(blocks // 2):
            theirs = slot_of[4 * (q // 2) + q % 2 + 2 * (1 - core)]
            for ch in range(4):
                send1[c, q, ch] = slots[ring, ch, theirs]
        copy1(c).start()
        for q in range(blocks // 2):
            mine = slot_of[4 * (q // 2) + q % 2 + 2 * core]
            for ch in range(4):
                keep1[c, q, ch] = slots[ring, ch, mine]

    def merge(c):
        copy1(c).wait_recv()

        def merged(q):
            return blend(
                [keep1[c, q, ch] for ch in range(4)],
                [recv1[c, q, ch] for ch in range(4)],
                core == 0,
            )

        for offset in (2, 1, 3):
            dest = lax.rem(chip + offset, 4)
            for i in range(2):
                for ch, value in enumerate(merged(2 * dest + i)):
                    send2[c, dest, i, ch] = value
            copy2(c, offset).start()
        for i in range(2):
            for ch, value in enumerate(merged(2 * chip + i)):
                recv2[c, 0, i, ch] = value

    def finish(t, carry):
        c = chunk_at(t)
        for offset in range(1, 4):
            copy2(c, offset).wait_recv()
        span = pl.ds(pl.multiple_of(c * chunk_rows, chunk_rows), chunk_rows)
        for i in range(2):
            value = None
            for source in (3, 2, 1, 0):
                offset = lax.rem(chip - source + 4, 4)
                part = [recv2[c, offset, i, ch] for ch in range(4)]
                if value is None:
                    value = part
                else:
                    value = [part[k] + part[3] * value[k] for k in range(3)] + [part[3] * value[3]]
            value[3] = 1.0 - value[3]
            for ch in range(4):
                out[ch, span, pl.ds(i * LANES, LANES)] = value[ch]
        return carry

    def march_window(t):
        def one(s, carry):
            march(window, t, s * GROUP, PAD + t * chunk_rows)
            return carry

        lax.fori_loop(0, SLOTS // GROUP, one, 0)

    peers = 4
    for condition in (has_far, has_up, has_down):
        peers = peers + jnp.where(condition, 1, 0)
    pl.semaphore_wait(barrier, peers)

    for side in range(2):

        @pl.when(z_sends[side])
        def _(side=side):
            flag_copy(side).start()

    def start_halo(t, carry):
        for side in range(2):

            @pl.when(z_sends[side])
            def _(side=side):
                z_copy(side, chunk_at(t)).start()

        return carry

    lax.fori_loop(0, CHUNKS, start_halo, 0)

    for copy in window_loads:
        copy.wait()
    for copy in loads:
        copy.start()
    march_window(0)
    march_window(1)

    for copy in loads:
        copy.wait()

    def pack(b, carry):
        flag = flags[pl.ds(b, 1), :]
        for z in range(cells):
            y_send[0, b, pl.ds(z, 1), :] = brick[b, z, pl.ds(PAD + rows - 1, 1), :] * flag
            y_send[1, b, pl.ds(z, 1), :] = brick[b, z, pl.ds(PAD, 1), :] * flag
        return carry

    lax.fori_loop(0, blocks, pack, 0)
    for side in range(2):

        @pl.when(y_sends[side])
        def _(side=side):
            y_copy(side).start()

        @pl.when(z_receives[side])
        def _(side=side):
            flag_copy(side).wait_recv()

    def one_chunk(t, carry):
        c = chunk_at(t)
        first_row = pl.multiple_of(c * chunk_rows, chunk_rows)
        for side in range(2):

            @pl.when(z_receives[side])
            def _(side=side):
                z_copy(side, c).wait_recv()
                for b in range(blocks):
                    edge = z_recv[side, pl.ds(first_row, chunk_rows), pl.ds(b * LANES, LANES)]
                    z_edge[side, b] = edge * z_flags[side, pl.ds(b, 1), :]

        ring = lax.rem(t, AHEAD + 1)
        row = pl.multiple_of(PAD + first_row, 8)

        def one_end(s, inner):
            ends(ring, s * GROUP, row)
            return inner

        lax.fori_loop(0, SLOTS // GROUP, one_end, 0)
        hand_over(c, ring)

        @pl.when(t == CHUNKS - 2 - AHEAD)
        def _():
            unpack()

        @pl.when(t + AHEAD < CHUNKS)
        def _():
            later_ring = lax.rem(t + AHEAD, AHEAD + 1)
            later_row = pl.multiple_of(PAD + chunk_at(t + AHEAD) * chunk_rows, 8)

            def one_slot(s, inner):
                march(brick, later_ring, s * GROUP, later_row)

                @pl.when(s == SLOTS // GROUP - 2)
                def _():
                    merge(c)

                return inner

            lax.fori_loop(0, SLOTS // GROUP, one_slot, 0)

        return carry

    lax.fori_loop(0, CHUNKS, one_chunk, 0)
    for t in range(CHUNKS - AHEAD, CHUNKS):
        merge(chunk_at(t))
    lax.fori_loop(0, CHUNKS, finish, 0)

    for side in range(2):

        @pl.when(z_sends[side])
        def _(side=side):
            flag_copy(side).wait_send()

        @pl.when(y_sends[side])
        def _(side=side):
            y_copy(side).wait_send()

    def drain(c, carry):
        for side in range(2):

            @pl.when(z_sends[side])
            def _(side=side):
                z_copy(side, c).wait_send()

        copy1(c).wait_send()
        for offset in range(1, 4):
            copy2(c, offset).wait_send()
        return carry

    lax.fori_loop(0, CHUNKS, drain, 0)


def solution(mesh):
    depth_n, rows_n = mesh.shape["depth"], mesh.shape["rows"]

    def shards(density, occupancy, transfer):
        cells, rows, columns = density.shape
        blocks = columns // LANES
        chunk_rows = rows // CHUNKS
        half = blocks // 2
        f32 = jnp.float32
        tile = (chunk_rows, LANES)
        dma = pltpu.SemaphoreType.DMA
        return pl.pallas_call(
            functools.partial(kernel, (cells, rows, blocks, depth_n, rows_n)),
            out_shape=jax.ShapeDtypeStruct((4, rows, columns // depth_n), f32),
            in_specs=[
                pl.BlockSpec(memory_space=pltpu.SMEM),
                pl.BlockSpec(memory_space=pltpu.SMEM),
                pl.BlockSpec(memory_space=pl.ANY),
            ],
            out_specs=pl.BlockSpec(memory_space=pltpu.VMEM),
            scratch_shapes=[
                pltpu.VMEM((blocks + 1, cells, rows + 2 * PAD, LANES), f32),
                pltpu.VMEM((blocks + 1, cells, AHEAD * chunk_rows + 2 * PAD, LANES), f32),
                pltpu.VMEM((2, rows, columns), f32),
                pltpu.VMEM((2, blocks) + tile, f32),
                pltpu.VMEM((blocks, LANES), f32),
                pltpu.VMEM((2, blocks, LANES), f32),
                pltpu.VMEM((2, blocks, cells, LANES), f32),
                pltpu.VMEM((2, blocks, cells, LANES), f32),
                pltpu.VMEM((AHEAD + 1, 4, SLOTS + 1) + tile, f32),
                pltpu.VMEM((CHUNKS, half, 4) + tile, f32),
                pltpu.VMEM((CHUNKS, half, 4) + tile, f32),
                pltpu.VMEM((CHUNKS, half, 4) + tile, f32),
                pltpu.VMEM((CHUNKS, 4, 2, 4) + tile, f32),
                pltpu.VMEM((CHUNKS, 4, 2, 4) + tile, f32),
                pltpu.SMEM((SLOTS,), jnp.int32),
                pltpu.SMEM((blocks,), jnp.int32),
                pltpu.SMEM((blocks,), jnp.int32),
                pltpu.SMEM((blocks,), jnp.int32),
                dma((blocks,)),
                dma((blocks,)),
                dma((2, 2, CHUNKS)),
                dma((2, 2)),
                dma((2, 2)),
                dma((2, CHUNKS)),
                dma((2, 3, CHUNKS)),
            ],
            compiler_params=pltpu.CompilerParams(
                collective_id=0,
                has_side_effects=True,
                vmem_limit_bytes=60 * 2**20,
            ),
        )(occupancy, transfer, density)

    return jax.shard_map(
        shards,
        mesh=mesh,
        in_specs=(P("depth", "rows", None), P("depth", "rows", None), P()),
        out_specs=P(None, "rows", "depth"),
        check_vma=False,
    )
```

```python
import functools

import jax
import jax.numpy as jnp
from jax import lax
from jax.experimental import pallas as pl
from jax.experimental.pallas import tpu as pltpu
from jax.sharding import PartitionSpec as P

MESH = pl.DeviceIdType.MESH
LOG2E = 1.4426950408889634
LANES = 128
PAD = 8
SLOTS = 12
CHUNKS = 8
AHEAD = 2
GROUP = 4
LIGHT_SCALE = 0.224
LIGHT_FLOOR = 0.15 / LIGHT_SCALE


def remote(src, dst, send_sem, recv_sem, **where):
    return pltpu.make_async_remote_copy(
        src_ref=src,
        dst_ref=dst,
        send_sem=send_sem,
        recv_sem=recv_sem,
        device_id=where,
        device_id_type=MESH,
    )


def blend(mine, theirs, mine_in_front):
    front = [jnp.where(mine_in_front, a, b) for a, b in zip(mine, theirs)]
    back = [jnp.where(mine_in_front, b, a) for a, b in zip(mine, theirs)]
    return [front[c] + front[3] * back[c] for c in range(3)] + [front[3] * back[3]]


def kernel(
    dims,
    occ_hbm,
    transfer_hbm,
    density,
    out,
    brick,
    window,
    z_recv,
    z_edge,
    flags,
    z_flags,
    y_send,
    y_recv,
    slots,
    send1,
    recv1,
    send2,
    recv2,
    slot_block,
    left_of,
    right_of,
    slot_of,
    occ,
    transfer,
    small_sem,
    load_sem,
    window_sem,
    z_sems,
    f_sems,
    y_sems,
    sems1,
    sems2,
):
    cells, rows, blocks, depth_n, rows_n = dims
    chunk_rows = rows // CHUNKS
    depth_at, row_at = lax.axis_index("depth"), lax.axis_index("rows")
    chip, core = depth_at // 2, depth_at % 2
    sibling = depth_at + 1 - 2 * core
    has_front, has_back = depth_at > 0, depth_at < depth_n - 1
    has_up, has_down = row_at > 0, row_at < rows_n - 1
    far = depth_at + 2 * core - 1
    has_far = jnp.logical_and(far >= 0, far < depth_n)

    small = [
        pltpu.make_async_copy(occ_hbm, occ, small_sem.at[0]),
        pltpu.make_async_copy(transfer_hbm, transfer, small_sem.at[1]),
    ]
    for copy in small:
        copy.start()
    barrier = pltpu.get_barrier_semaphore()

    def greet(**where):
        pl.semaphore_signal(barrier, inc=1, device_id=where, device_id_type=MESH)

    greet(depth=sibling)
    for offset in range(1, 4):
        greet(depth=lax.rem(depth_at + 2 * offset, depth_n))

    @pl.when(has_far)
    def _():
        greet(depth=far)

    @pl.when(has_up)
    def _():
        greet(rows=row_at - 1)

    @pl.when(has_down)
    def _():
        greet(rows=row_at + 1)

    window_row = chunk_rows - PAD
    window_loads = [
        pltpu.make_async_copy(
            density.at[:, pl.ds(window_row, window.shape[2]), pl.ds(LANES * b, LANES)],
            window.at[b],
            window_sem.at[b],
        )
        for b in range(blocks)
    ]
    loads = [
        pltpu.make_async_copy(
            density.at[:, :, pl.ds(LANES * b, LANES)],
            brick.at[b, :, pl.ds(PAD, rows), :],
            load_sem.at[b],
        )
        for b in range(blocks)
    ]
    for copy in window_loads:
        copy.start()

    for copy in small:
        copy.wait()

    for b in range(blocks):
        flags[pl.ds(b, 1), :] = jnp.full((1, LANES), occ[0, 0, b], jnp.int32).astype(jnp.float32)

    def chunk_at(t):
        return lax.rem(t + 1, CHUNKS)

    def z_copy(side, c):
        span = pl.ds(pl.multiple_of(c * chunk_rows, chunk_rows), chunk_rows)
        return remote(
            density.at[cells - 1 if side == 0 else 0, span, :],
            z_recv.at[side, span, :],
            z_sems.at[0, side, c],
            z_sems.at[1, side, c],
            depth=depth_at + 1 if side == 0 else depth_at - 1,
        )

    def flag_copy(side):
        return remote(
            flags,
            z_flags.at[side],
            f_sems.at[0, side],
            f_sems.at[1, side],
            depth=depth_at + 1 if side == 0 else depth_at - 1,
        )

    def y_copy(side):
        return remote(
            y_send.at[side],
            y_recv.at[side],
            y_sems.at[0, side],
            y_sems.at[1, side],
            rows=row_at + 1 if side == 0 else row_at - 1,
        )

    z_sends, z_receives = (has_back, has_front), (has_front, has_back)
    y_sends, y_receives = (has_down, has_up), (has_up, has_down)

    occupied = [occ[0, 0, b] for b in range(blocks)]
    before, count = [], jnp.int32(0)
    for b in range(blocks):
        before.append(count)
        count = count + occupied[b]
    for s in range(SLOTS):
        found = jnp.int32(0)
        for b in range(1, blocks):
            hit = jnp.logical_and(occupied[b] == 1, before[b] == s)
            found = jnp.where(hit, b, found)
        slot_block[s] = found
    for b in range(blocks):
        slot_of[b] = jnp.where(occupied[b] == 1, before[b], SLOTS)
        left_of[b] = blocks if b == 0 else jnp.where(occupied[b - 1] == 1, b - 1, blocks)
        right_of[b] = (
            blocks if b == blocks - 1 else jnp.where(occupied[b + 1] == 1, b + 1, blocks)
        )

    def clear(z, carry):
        brick[blocks, z] = jnp.zeros(brick.shape[2:], jnp.float32)
        window[blocks, z] = jnp.zeros(window.shape[2:], jnp.float32)
        return carry

    lax.fori_loop(0, cells, clear, 0)
    for r in range(AHEAD + 1):
        for c in range(4):
            slots[r, c, SLOTS] = jnp.full((chunk_rows, LANES), float(c == 3), jnp.float32)
    for side in range(2):

        @pl.when(jnp.logical_not(z_receives[side]))
        def _(side=side):
            z_edge[side] = jnp.zeros(z_edge.shape[1:], jnp.float32)

    halo_row = (PAD - 1, PAD + rows)

    def unpack():
        for side in range(2):

            @pl.when(y_receives[side])
            def _(side=side):
                y_copy(side).wait_recv()

                def one(b, carry):
                    for z in range(cells):
                        brick[b, z, pl.ds(halo_row[side], 1), :] = y_recv[side, b, pl.ds(z, 1), :]
                    return carry

                lax.fori_loop(0, blocks, one, 0)

            @pl.when(jnp.logical_not(y_receives[side]))
            def _(side=side):
                def one(b, carry):
                    for z in range(cells):
                        brick[b, z, pl.ds(halo_row[side], 1), :] = jnp.zeros(
                            (1, LANES), jnp.float32
                        )
                    return carry

                lax.fori_loop(0, blocks, one, 0)

    lane = lax.broadcasted_iota(jnp.int32, (chunk_rows, LANES), 1)
    first_lane, last_lane = lane == 0, lane == LANES - 1
    ext_slope, ext_offset = transfer[0, 3] * LOG2E, transfer[1, 3] * LOG2E
    step_scale = -2.0 / (cells * depth_n) * LOG2E
    channels = [(transfer[0, c] * 0.5, transfer[1, c] * 0.5) for c in range(3)]

    def shade(center, diff_z, diff_y, beside_left, beside_right, transmit):
        after = pltpu.roll(jnp.where(first_lane, beside_right, center), LANES - 1, 1)
        ahead = pltpu.roll(jnp.where(last_lane, beside_left, center), 1, 1)
        diff_x = after - ahead
        slope = jnp.abs(0.75 * diff_z + 0.9375 * diff_y + diff_x)
        norm = diff_x * diff_x + diff_y * diff_y + (diff_z * diff_z + 4.0)
        lighting = LIGHT_FLOOR + slope * lax.rsqrt(norm)
        grown = 1.0 + jnp.exp2(ext_slope * center + ext_offset)
        factor = jnp.exp2((step_scale * center) * jnp.log(grown))
        kept = factor if transmit is None else transmit * factor
        weight = ((1.0 if transmit is None else transmit) - kept) * lighting
        return kept, weight, [jnp.tanh(slope_c * center + offset_c) for slope_c, offset_c in channels]

    def cell_rows(ref, b, z, row):
        return ref[b, z, pl.ds(row, chunk_rows), :]

    def layer(ref, b, z, row, center, diff_z, transmit):
        diff_y = cell_rows(ref, b, z, row + 1) - cell_rows(ref, b, z, row - 1)
        return shade(
            center,
            diff_z,
            diff_y,
            cell_rows(ref, left_of[b], z, row),
            cell_rows(ref, right_of[b], z, row),
            transmit,
        )

    def march(ref, ring, first_slot, row):
        group = range(GROUP)
        block = [slot_block[first_slot + g] for g in group]
        previous = [cell_rows(ref, block[g], 0, row) for g in group]
        center = [cell_rows(ref, block[g], 1, row) for g in group]
        transmit, total, sums = [None] * GROUP, [None] * GROUP, [None] * GROUP
        for z in range(1, cells - 1):
            for g in group:
                following = cell_rows(ref, block[g], z + 1, row)
                kept, weight, factors = layer(
                    ref, block[g], z, row, center[g], following - previous[g], transmit[g]
                )
                products = [weight * f for f in factors]
                if total[g] is None:
                    total[g], sums[g] = weight, products
                else:
                    total[g] = total[g] + weight
                    sums[g] = [a + b for a, b in zip(sums[g], products)]
                transmit[g] = kept
                previous[g], center[g] = center[g], following
        for g in group:
            for c in range(3):
                slots[ring, c, first_slot + g] = LIGHT_SCALE * (total[g] + sums[g][c])
            slots[ring, 3, first_slot + g] = transmit[g]

    def ends(ring, first_slot, row):
        for g in range(GROUP):
            s = first_slot + g
            b = slot_block[s]
            color = [slots[ring, c, s] for c in range(3)]
            last = cells - 1
            center = cell_rows(brick, b, 0, row)
            diff_z = cell_rows(brick, b, 1, row) - z_edge[0, b]
            kept, weight, factors = layer(brick, b, 0, row, center, diff_z, None)
            weight = weight * LIGHT_SCALE
            color = [(weight + weight * f) + kept * c for f, c in zip(factors, color)]
            transmit = kept * slots[ring, 3, s]
            center = cell_rows(brick, b, last, row)
            diff_z = z_edge[1, b] - cell_rows(brick, b, last - 1, row)
            kept, weight, factors = layer(brick, b, last, row, center, diff_z, transmit)
            weight = weight * LIGHT_SCALE
            for c in range(3):
                slots[ring, c, s] = color[c] + (weight + weight * factors[c])
            slots[ring, 3, s] = kept

    def copy1(c):
        return remote(
            send1.at[c], recv1.at[c], sems1.at[0, c], sems1.at[1, c], depth=sibling
        )

    def copy2(c, offset):
        dest = lax.rem(chip + offset, 4)
        return remote(
            send2.at[c, dest],
            recv2.at[c, offset],
            sems2.at[0, offset - 1, c],
            sems2.at[1, offset - 1, c],
            depth=2 * dest + core,
        )

    def hand_over(c, ring):
        for q in range(blocks // 2):
            theirs = slot_of[4 * (q // 2) + q % 2 + 2 * (1 - core)]
            for ch in range(4):
                send1[c, q, ch] = slots[ring, ch, theirs]
        copy1(c).start()

    def merge(c, ring):
        copy1(c).wait_recv()

        def merged(q):
            mine = slot_of[4 * (q // 2) + q % 2 + 2 * core]
            return blend(
                [slots[ring, ch, mine] for ch in range(4)],
                [recv1[c, q, ch] for ch in range(4)],
                core == 0,
            )

        for offset in (2, 1, 3):
            dest = lax.rem(chip + offset, 4)
            for i in range(2):
                for ch, value in enumerate(merged(2 * dest + i)):
                    send2[c, dest, i, ch] = value
            copy2(c, offset).start()
        for i in range(2):
            for ch, value in enumerate(merged(2 * chip + i)):
                recv2[c, 0, i, ch] = value

    def finish(t, carry):
        c = chunk_at(t)
        for offset in range(1, 4):
            copy2(c, offset).wait_recv()
        span = pl.ds(pl.multiple_of(c * chunk_rows, chunk_rows), chunk_rows)
        for i in range(2):
            value = None
            for source in (3, 2, 1, 0):
                offset = lax.rem(chip - source + 4, 4)
                part = [recv2[c, offset, i, ch] for ch in range(4)]
                if value is None:
                    value = part
                else:
                    value = [part[k] + part[3] * value[k] for k in range(3)] + [part[3] * value[3]]
            value[3] = 1.0 - value[3]
            for ch in range(4):
                out[ch, span, pl.ds(i * LANES, LANES)] = value[ch]
        return carry

    def march_window(t):
        def one(s, carry):
            march(window, t, s * GROUP, PAD + t * chunk_rows)
            return carry

        lax.fori_loop(0, SLOTS // GROUP, one, 0)

    peers = 4
    for condition in (has_far, has_up, has_down):
        peers = peers + jnp.where(condition, 1, 0)
    pl.semaphore_wait(barrier, peers)

    for side in range(2):

        @pl.when(z_sends[side])
        def _(side=side):
            flag_copy(side).start()

    def start_halo(t, carry):
        for side in range(2):

            @pl.when(z_sends[side])
            def _(side=side):
                z_copy(side, chunk_at(t)).start()

        return carry

    lax.fori_loop(0, CHUNKS, start_halo, 0)

    for copy in window_loads:
        copy.wait()
    for copy in loads:
        copy.start()
    march_window(0)
    for t in range(1, AHEAD):
        march_window(t)

    for copy in loads:
        copy.wait()

    def pack(b, carry):
        flag = flags[pl.ds(b, 1), :]
        for z in range(cells):
            y_send[0, b, pl.ds(z, 1), :] = brick[b, z, pl.ds(PAD + rows - 1, 1), :] * flag
            y_send[1, b, pl.ds(z, 1), :] = brick[b, z, pl.ds(PAD, 1), :] * flag
        return carry

    lax.fori_loop(0, blocks, pack, 0)
    for side in range(2):

        @pl.when(y_sends[side])
        def _(side=side):
            y_copy(side).start()

        @pl.when(z_receives[side])
        def _(side=side):
            flag_copy(side).wait_recv()

    def one_chunk(t, carry):
        c = chunk_at(t)
        first_row = pl.multiple_of(c * chunk_rows, chunk_rows)
        for side in range(2):

            @pl.when(z_receives[side])
            def _(side=side):
                z_copy(side, c).wait_recv()
                for b in range(blocks):
                    edge = z_recv[side, pl.ds(first_row, chunk_rows), pl.ds(b * LANES, LANES)]
                    z_edge[side, b] = edge * z_flags[side, pl.ds(b, 1), :]

        ring = lax.rem(t, AHEAD + 1)
        row = pl.multiple_of(PAD + first_row, 8)

        def one_end(s, inner):
            ends(ring, s * GROUP, row)
            return inner

        lax.fori_loop(0, SLOTS // GROUP, one_end, 0)
        hand_over(c, ring)

        @pl.when(t == CHUNKS - 2 - AHEAD)
        def _():
            unpack()

        @pl.when(t + AHEAD < CHUNKS)
        def _():
            later_ring = lax.rem(t + AHEAD, AHEAD + 1)
            later_row = pl.multiple_of(PAD + chunk_at(t + AHEAD) * chunk_rows, 8)

            def one_slot(s, inner):
                march(brick, later_ring, s * GROUP, later_row)

                @pl.when(s == SLOTS // GROUP - 1)
                def _():
                    merge(c, ring)

                return inner

            lax.fori_loop(0, SLOTS // GROUP, one_slot, 0)

        return carry

    lax.fori_loop(0, CHUNKS, one_chunk, 0)
    for t in range(CHUNKS - AHEAD, CHUNKS):
        merge(chunk_at(t), t % (AHEAD + 1))
    lax.fori_loop(0, CHUNKS, finish, 0)

    for side in range(2):

        @pl.when(z_sends[side])
        def _(side=side):
            flag_copy(side).wait_send()

        @pl.when(y_sends[side])
        def _(side=side):
            y_copy(side).wait_send()

    def drain(c, carry):
        for side in range(2):

            @pl.when(z_sends[side])
            def _(side=side):
                z_copy(side, c).wait_send()

        copy1(c).wait_send()
        for offset in range(1, 4):
            copy2(c, offset).wait_send()
        return carry

    lax.fori_loop(0, CHUNKS, drain, 0)


def solution(mesh):
    depth_n, rows_n = mesh.shape["depth"], mesh.shape["rows"]

    def shards(density, occupancy, transfer):
        cells, rows, columns = density.shape
        blocks = columns // LANES
        chunk_rows = rows // CHUNKS
        half = blocks // 2
        f32 = jnp.float32
        tile = (chunk_rows, LANES)
        dma = pltpu.SemaphoreType.DMA
        return pl.pallas_call(
            functools.partial(kernel, (cells, rows, blocks, depth_n, rows_n)),
            out_shape=jax.ShapeDtypeStruct((4, rows, columns // depth_n), f32),
            in_specs=[
                pl.BlockSpec(memory_space=pltpu.HBM),
                pl.BlockSpec(memory_space=pltpu.HBM),
                pl.BlockSpec(memory_space=pltpu.HBM),
            ],
            out_specs=pl.BlockSpec(memory_space=pltpu.VMEM),
            scratch_shapes=[
                pltpu.VMEM((blocks + 1, cells, rows + 2 * PAD, LANES), f32),
                pltpu.VMEM((blocks + 1, cells, AHEAD * chunk_rows + 2 * PAD, LANES), f32),
                pltpu.VMEM((2, rows, columns), f32),
                pltpu.VMEM((2, blocks) + tile, f32),
                pltpu.VMEM((blocks, LANES), f32),
                pltpu.VMEM((2, blocks, LANES), f32),
                pltpu.VMEM((2, blocks, cells, LANES), f32),
                pltpu.VMEM((2, blocks, cells, LANES), f32),
                pltpu.VMEM((AHEAD + 1, 4, SLOTS + 1) + tile, f32),
                pltpu.VMEM((CHUNKS, half, 4) + tile, f32),
                pltpu.VMEM((CHUNKS, half, 4) + tile, f32),
                pltpu.VMEM((CHUNKS, 4, 2, 4) + tile, f32),
                pltpu.VMEM((CHUNKS, 4, 2, 4) + tile, f32),
                pltpu.SMEM((SLOTS,), jnp.int32),
                pltpu.SMEM((blocks,), jnp.int32),
                pltpu.SMEM((blocks,), jnp.int32),
                pltpu.SMEM((blocks,), jnp.int32),
                pltpu.SMEM((1, 1, blocks), jnp.int32),
                pltpu.SMEM((2, 4), f32),
                dma((2,)),
                dma((blocks,)),
                dma((blocks,)),
                dma((2, 2, CHUNKS)),
                dma((2, 2)),
                dma((2, 2)),
                dma((2, CHUNKS)),
                dma((2, 3, CHUNKS)),
            ],
            compiler_params=pltpu.CompilerParams(
                collective_id=0,
                has_side_effects=True,
                vmem_limit_bytes=44 * 2**20,
            ),
        )(occupancy, transfer, density)

    return jax.shard_map(
        shards,
        mesh=mesh,
        in_specs=(P("depth", "rows", None), P("depth", "rows", None), P()),
        out_specs=P(None, "rows", "depth"),
        check_vma=False,
    )
```
